32 devices in a mesh: fsdp: 4 (over x, core), chan: 8 (over z, y).
Axes of the slice: x: 2, y: 2, z: 4, core: 2. Of those that a mesh axis runs over, the one named last changes fastest.
Arguments:
- hidden: bfloat16 [512, 4096], P('fsdp'), may hold values from -6 to 6
- conv_out: bfloat16 [512, 8192], P('fsdp', 'chan'), may hold values from -6 to 6
- state_in: float32 [8192, 16], P('chan'), may hold values from -6 to 6
- gate_weight: bfloat16 [4096, 8192], P('fsdp', 'chan'), may hold values from -0.09375 to 0.09375
- xproj_weight: bfloat16 [8192, 288], P('chan'), may hold values from -0.0625 to 0.0625
- dt_weight: bfloat16 [256, 8192], P(None, 'chan'), may hold values from -0.375 to 0.375
- dt_bias: float32 [8192], P('chan'), may hold values from -7 to -1
- a_log: float32 [8192, 16], P('chan'), may hold values from -1.5 to 2.77
- skip_gain: float32 [8192], P('chan'), may hold values from 0.25 to 1
- out_weight: bfloat16 [4096, 8192], P('fsdp', 'chan'), may hold values from -0.0625 to 0.0625
Outputs:
- mixed: bfloat16 [512, 4096], P(('fsdp', 'chan'))
The draws below stay inside these ranges and needn't reach their ends.
All inputs are finite; a program needn't handle non-finite values.
Results may differ from the reference program's by a relative error of at most 0.007.
Values may be sent and summed in bfloat16 or wider, within the bound.
A program may use at most 64 MiB of HBM per device.

```python
import jax
import jax.numpy as jnp
from jax import lax

D = 4096
INNER = 8192
STATE = 16
RANK = 256
LENGTH = 512
PROJ = 288


def levels(rng, extent, split, least, top_value):
    level = 1.0
    for dim, blocks in split:
        draws = jax.random.uniform(jax.random.fold_in(jax.random.fold_in(rng, 6), dim), (blocks,), jnp.float32, least / len(split), top_value / len(split))
        level = level * jnp.repeat(jnp.exp(draws), extent[dim] // blocks).reshape((-1,) + (1,) * (len(extent) - 1 - dim))
    return level


def centred(own_key, shape, scale, most, shards=(), kind=jnp.bfloat16):
    result = scale * jax.random.normal(own_key, shape, jnp.float32)
    if shards:
        result = result * levels(own_key, shape, shards, -0.22, 0.18)
    return jnp.clip(result, -most, most).astype(kind)


def setup_inputs(seed: int = 0) -> dict:
    arg_keys = jax.random.split(jax.random.key(seed), 11)
    hidden = centred(arg_keys[0], (LENGTH, D), 1.0, 6.0, ((0, 4),))
    conv_out = centred(arg_keys[1], (LENGTH, INNER), 1.0, 6.0, ((0, 4), (1, 8)))
    state_in = centred(arg_keys[2], (INNER, STATE), 1.0, 6.0, ((0, 8),), jnp.float32)
    gate_weight = centred(arg_keys[3], (D, INNER), D ** -0.5, 0.09375, ((0, 4), (1, 8)))
    xproj_weight = centred(arg_keys[4], (INNER, PROJ), INNER ** -0.5, 0.0625, ((0, 8),))
    dt_weight = centred(arg_keys[5], (RANK, INNER), RANK ** -0.5, 0.375, ((1, 8),))
    dt_bias = jnp.clip(-7.0 + 6.0 * jax.random.uniform(arg_keys[6], (INNER,), jnp.float32) ** levels(arg_keys[6], (INNER,), ((0, 8),), -0.2, 0.2), -7.0, -1.0)
    a_log = jnp.clip(-1.5 + 4.27 * jax.random.uniform(arg_keys[7], (INNER, STATE), jnp.float32) ** levels(arg_keys[7], (INNER, STATE), ((0, 8),), -0.2, 0.2), -1.5, 2.77)
    skip_gain = jnp.clip(0.25 + 0.75 * jax.random.uniform(arg_keys[8], (INNER,), jnp.float32) ** levels(arg_keys[8], (INNER,), ((0, 8),), -0.2, 0.2), 0.25, 1.0)
    out_weight = centred(arg_keys[9], (D, INNER), INNER ** -0.5, 0.0625, ((0, 4), (1, 8)))
    return {"hidden": hidden, "conv_out": conv_out, "state_in": state_in, "gate_weight": gate_weight, "xproj_weight": xproj_weight, "dt_weight": dt_weight, "dt_bias": dt_bias, "a_log": a_log, "skip_gain": skip_gain, "out_weight": out_weight}


def reference(hidden, conv_out, state_in, gate_weight, xproj_weight, dt_weight, dt_bias, a_log, skip_gain, out_weight):
    gate_pre = jnp.dot(hidden, gate_weight, preferred_element_type=jnp.float32)
    projected = jnp.dot(conv_out, xproj_weight, preferred_element_type=jnp.float32)
    step_low = projected[:, :RANK].astype(jnp.bfloat16)
    in_coef = projected[:, RANK:RANK + STATE]
    out_coef = projected[:, RANK + STATE:]
    step_size = jax.nn.softplus(jnp.dot(step_low, dt_weight, preferred_element_type=jnp.float32) + dt_bias)
    decay_rate = -jnp.exp(a_log)
    inputs = conv_out.astype(jnp.float32)

    def advance(carry_state, step_items):
        step_row, input_row, in_row, out_row = step_items
        carry_state = jnp.exp(step_row[:, None] * decay_rate) * carry_state + (step_row * input_row)[:, None] * in_row[None, :]
        return carry_state, jnp.sum(carry_state * out_row[None, :], axis=1)

    last_state, scanned = lax.scan(advance, state_in, (step_size, inputs, in_coef, out_coef))
    gated = ((scanned + skip_gain * inputs) * jax.nn.silu(gate_pre)).astype(jnp.bfloat16)
    mixed = lax.dot_general(gated, out_weight, (((1,), (1,)), ((), ())), preferred_element_type=jnp.float32)
    return mixed.astype(jnp.bfloat16)
```

```python
import functools

import jax
import jax.numpy as jnp
from jax import lax
from jax.experimental import pallas as pl
from jax.experimental.pallas import tpu as pltpu
from jax.sharding import PartitionSpec as P

STATE = 16
RANK = 256
BLOCK = 16


def running_sum(values):
    lower = jnp.tril(jnp.ones((values.shape[0],) * 2, jnp.float32))
    return jnp.dot(lower, values, precision=lax.Precision.HIGHEST)


def generic_shards(
    hidden,
    conv_out,
    state_in,
    gate_weight,
    xproj_weight,
    dt_weight,
    dt_bias,
    a_log,
    skip_gain,
    out_weight,
):
    rows_here, channels = conv_out.shape
    partial_value = jnp.dot(conv_out, xproj_weight, preferred_element_type=jnp.float32)
    projected = lax.psum(partial_value, "chan")
    step_low = projected[:, :RANK].astype(jnp.bfloat16)
    in_coef = projected[:, RANK : RANK + STATE]
    out_coef = projected[:, RANK + STATE :]
    step_size = jax.nn.softplus(
        jnp.dot(step_low, dt_weight, preferred_element_type=jnp.float32) + dt_bias
    )
    decay_rate = -jnp.exp(a_log)
    inputs = conv_out.astype(jnp.float32)
    blocks = rows_here // BLOCK
    position_rows = lax.broadcasted_iota(jnp.int32, (BLOCK, BLOCK), 0)
    position_cols = lax.broadcasted_iota(jnp.int32, (BLOCK, BLOCK), 1)
    causal_mask = position_rows >= position_cols

    def block_step(carry_state, block_items):
        step_blk, input_blk, in_blk, out_blk = block_items
        within = running_sum(step_blk)
        spread = jnp.where(causal_mask[:, :, None], within[:, None, :] - within[None, :, :], 0.0)
        weights = jnp.where(
            causal_mask[:, :, None, None], jnp.exp(spread[:, :, :, None] * decay_rate), 0.0
        )
        driven = (step_blk * input_blk)[:, :, None] * in_blk[:, None, :]
        states = jnp.einsum("tscn,scn->tcn", weights, driven, precision=lax.Precision.HIGHEST)
        states = states + jnp.exp(within[:, :, None] * decay_rate) * carry_state[None]
        block_out = jnp.einsum("tcn,tn->tc", states, out_blk, precision=lax.Precision.HIGHEST)
        return (states[-1], block_out)

    def split_blocks(values):
        return values.reshape((blocks, BLOCK) + values.shape[1:])

    empty_state = jnp.zeros((channels, STATE), jnp.float32)
    last_state, local_out = lax.scan(
        block_step,
        empty_state,
        (
            split_blocks(step_size),
            split_blocks(inputs),
            split_blocks(in_coef),
            split_blocks(out_coef),
        ),
    )
    local_out = local_out.reshape((rows_here, channels))
    total_step = jnp.sum(step_size, axis=0)
    totals, finals = (
        lax.all_gather(total_step[None], "fsdp", axis=0, tiled=True),
        lax.all_gather(last_state[None], "fsdp", axis=0, tiled=True),
    )
    position = lax.axis_index("fsdp")
    sources = jnp.arange(totals.shape[0], dtype=jnp.int32)
    earlier_mask = sources < position
    through_sum = running_sum(totals)
    before_sum = jnp.sum(jnp.where(earlier_mask[:, None], totals, 0.0), axis=0)
    gap_steps = jnp.where(earlier_mask[:, None], before_sum[None, :] - through_sum, 0.0)
    factor = jnp.where(
        earlier_mask[:, None, None], jnp.exp(gap_steps[:, :, None] * decay_rate), 0.0
    )
    entering = (
        jnp.sum(factor * finals, axis=0) + jnp.exp(before_sum[:, None] * decay_rate) * state_in
    )
    through = running_sum(step_size)
    carried = jnp.einsum(
        "tcn,tn->tc",
        jnp.exp(through[:, :, None] * decay_rate) * entering[None],
        out_coef,
        precision=lax.Precision.HIGHEST,
    )
    scanned = local_out + carried
    gate_full, out_full = (
        lax.all_gather(gate_weight, "fsdp", axis=0, tiled=True),
        lax.all_gather(out_weight, "fsdp", axis=0, tiled=True),
    )
    gate_pre = jnp.dot(hidden, gate_full, preferred_element_type=jnp.float32)
    gated_out = ((scanned + skip_gain * inputs) * jax.nn.silu(gate_pre)).astype(jnp.bfloat16)
    summed = lax.psum_scatter(
        lax.dot_general(
            gated_out, out_full, (((1,), (1,)), ((), ())), preferred_element_type=jnp.float32
        ),
        "chan",
        scatter_dimension=0,
        tiled=True,
    )
    mixed = summed.astype(jnp.bfloat16)
    return mixed


LANES = 128
STEPS = 16


def fused_kernel(
    F,
    G,
    hidden,
    conv,
    state,
    gate_w,
    xproj,
    dt_w,
    dt_bias,
    a_log,
    skip,
    out_w,
    out,
    pp,
    pp_in,
    conv_in,
    hid_in,
    pg,
    gate_send,
    gate_own,
    gate_in,
    steps_s,
    drive_s,
    tiled_s,
    y_s,
    gated,
    po,
    fin_in,
    pp_ss,
    pp_rs,
    cv_ss,
    cv_rs,
    hd_ss,
    hd_rs,
    pg_ss,
    pg_rs,
    gt_ss,
    gt_rs,
    gd_ss,
    gd_rs,
    fo_ss,
    fo_rs,
):
    f32, bf16 = jnp.float32, jnp.bfloat16
    N = F * G
    f, c = lax.axis_index("fsdp"), lax.axis_index("chan")
    me = f * G + c
    rows, channels = conv.shape
    R, CS, DB = rows // G, channels // F, gate_w.shape[0]
    wide = pp.shape[1]

    def remote(src, dst, ss, rs, f2, c2):
        return pltpu.make_async_remote_copy(
            src_ref=src,
            dst_ref=dst,
            send_sem=ss,
            recv_sem=rs,
            device_id={"fsdp": f2, "chan": c2},
            device_id_type=pl.DeviceIdType.MESH,
        )

    def at(base, size, step):
        return pl.ds(pl.multiple_of(base * step, step), size)

    barrier = pltpu.get_barrier_semaphore()

    @pl.loop(1, N)
    def _(p):
        lin = lax.rem(me + p, N)
        pl.semaphore_signal(
            barrier,
            inc=1,
            device_id={"fsdp": lin // G, "chan": lax.rem(lin, G)},
            device_id_type=pl.DeviceIdType.MESH,
        )

    pp[:, RANK:] = jnp.zeros((rows, wide - RANK), f32)
    pp[:, : xproj.shape[1]] = jnp.dot(conv[...], xproj[...], preferred_element_type=f32)
    pl.semaphore_wait(barrier, N - 1)

    def pp_copy(j):
        c2 = lax.rem(c + j, G)
        return remote(pp.at[at(c2, R, R)], pp_in.at[c], pp_ss.at[c2], pp_rs.at[c], f, c2)

    def conv_copy(f2):
        return remote(conv.at[:, at(f2, CS, CS)], conv_in.at[f], cv_ss.at[f2], cv_rs.at[f], f2, c)

    def hid_copy(f2):
        return remote(hidden.at[:, at(f2, DB, DB)], hid_in.at[f], hd_ss.at[f2], hd_rs.at[f], f2, c)

    pl.loop(1, G)(lambda j: pp_copy(j).start())
    for j in range(1, F):
        hid_copy(lax.rem(f + j, F)).start()
        conv_copy(lax.rem(f + j, F)).start()
    conv_in[f] = conv[:, at(f, CS, CS)]
    hid_in[f] = hidden[:, at(f, DB, DB)]

    def gate_copy(k, f2):
        piece = at(k, rows, rows)
        return remote(
            gate_send.at[f2, piece], gate_in.at[f, piece], gt_ss.at[k * F + f2], gt_rs.at[k * F + f], f2, c
        )

    def gate_block(k):
        piece = at(k, rows, rows)
        lhs = hid_in[k]
        for j in range(F):
            f2 = lax.rem(f + j, F)
            part = jnp.dot(lhs, gate_w[:, at(f2, CS, CS)], preferred_element_type=f32)
            if j == 0:
                gate_own[piece] = part
            else:
                gate_send[f2, piece] = part.astype(bf16)
                gate_copy(k, f2).start()

    gate_block(f)

    total = pp[at(c, R, R)]
    for j in range(1, G):
        c2 = lax.rem(c + j, G)
        remote(pp.at[at(c, R, R)], pp_in.at[c2], pp_ss.at[c2], pp_rs.at[c2], f, c2).wait_recv()
        total = total + pp_in[c2]
    high = total.astype(bf16)
    low = (total[:, RANK:] - high[:, RANK:].astype(f32)).astype(bf16)
    pg[at(me, R, R), :wide] = high
    pg[at(me, R, R), wide:] = low

    def pg_copy(f2, c2):
        mine = pg.at[at(me, R, R)]
        lin = f2 * G + c2
        return remote(mine, mine, pg_ss.at[lin], pg_rs.at[me], f2, c2)

    @pl.loop(1, N)
    def _(p):
        lin = lax.rem(me + p, N)
        pg_copy(lin // G, lax.rem(lin, G)).start()

    decay = -jnp.exp(a_log[at(f, CS, CS), :].T)
    bias = dt_bias[:, at(f, CS, CS)]
    gain = skip[:, at(f, CS, CS)]
    weight = dt_w[:, at(f, CS, CS)]
    span = STEPS * STATE
    r_id = lax.broadcasted_iota(jnp.int32, (LANES, 2 * span), 0)
    q_id = lax.broadcasted_iota(jnp.int32, (LANES, 2 * span), 1)
    spread = (r_id == (q_id // span) * STATE + q_id % STATE).astype(bf16)
    own = (
        lax.broadcasted_iota(jnp.int32, (STEPS, span), 1) // STATE
        == lax.broadcasted_iota(jnp.int32, (STEPS, span), 0)
    )

    def scan_block(k, h):
        for j in range(G):
            @pl.when(k * G + j != me)
            def _():
                there = pg.at[at(k * G + j, R, R)]
                remote(there, there, pg_ss.at[k * G + j], pg_rs.at[k * G + j], k, j).wait_recv()

        @pl.when(k != f)
        def _():
            remote(conv.at[:, at(k, CS, CS)], conv_in.at[k], cv_ss.at[k], cv_rs.at[k], k, c).wait_recv()

        piece = at(k, rows, rows)
        raw = jnp.dot(pg[piece, :RANK], weight, preferred_element_type=f32) + bias
        size = jnp.maximum(raw, 0.0) + jnp.log1p(jnp.exp(-jnp.abs(raw)))
        steps_s[...] = size
        drive_s[...] = size * conv_in[k].astype(f32)
        tiled_s[:, : 2 * span] = jnp.dot(pg[piece, RANK:wide], spread, preferred_element_type=f32)
        tiled_s[:, 2 * span :] = jnp.dot(pg[piece, wide:], spread, preferred_element_type=f32)

        def sub(b, h):
            sl = at(b, STEPS, STEPS)
            dt = steps_s[sl]
            u = drive_s[sl]
            u_hi = u.astype(bf16)
            u_lo = (u - u_hi.astype(f32)).astype(bf16)

            def diagonal(i):
                return jnp.where(own, tiled_s[sl, i * span : (i + 1) * span], 0.0).astype(bf16)

            b_hi, c_hi, b_lo, c_lo = (diagonal(i) for i in range(4))
            driven = lax.dot_general(
                jnp.concatenate([b_hi, b_hi, b_lo], axis=0),
                jnp.concatenate([u_hi, u_lo, u_hi], axis=0),
                (((0,), (0,)), ((), ())),
                preferred_element_type=f32,
            )
            hs = []
            for s in range(STEPS):
                a = jnp.exp(dt[s : s + 1] * decay)
                h = a * h + driven[s * STATE : (s + 1) * STATE]
                hs.append(h.astype(bf16))
            both = jnp.dot(
                jnp.concatenate([c_hi, c_lo], axis=0),
                jnp.concatenate(hs, axis=0),
                preferred_element_type=f32,
            )
            y_s[at(k * (rows // STEPS) + b, STEPS, STEPS)] = both[:STEPS] + both[STEPS:]
            return h

        return lax.fori_loop(0, rows // STEPS, sub, h)

    def scan_and_gate(k, h):
        h = scan_block(k, h)

        @pl.when(k < F - 1)
        def _():
            g = lax.rem(f + 1 + k, F)
            remote(hidden.at[:, at(g, DB, DB)], hid_in.at[g], hd_ss.at[g], hd_rs.at[g], g, c).wait_recv()
            gate_block(g)

        return h

    lax.fori_loop(0, F, scan_and_gate, state[at(f, CS, CS), :].T)

    def gated_copy(k, f2):
        mine = gated.at[at(k, rows, rows), at(f, CS, CS)]
        return remote(mine, mine, gd_ss.at[k * F + f2], gd_rs.at[k * F + f], f2, c)

    @pl.loop(0, F)
    def _(k):
        piece = at(k, rows, rows)
        pre = gate_own[piece]
        for j in range(1, F):
            f2 = lax.rem(f + j, F)
            remote(
                gate_send.at[f2, piece], gate_in.at[f2, piece], gt_ss.at[k * F + f2], gt_rs.at[k * F + f2], f2, c
            ).wait_recv()
            pre = pre + gate_in[f2, piece].astype(f32)
        scanned = y_s[piece] + gain * conv_in[k].astype(f32)
        gated[piece, at(f, CS, CS)] = (scanned * (pre / (1.0 + jnp.exp(-pre)))).astype(bf16)
        for j in range(1, F):
            gated_copy(k, lax.rem(f + j, F)).start()

    def out_copy(k, c2):
        lin = k * G + c2
        return remote(po.at[at(lin, R, R)], fin_in.at[me], fo_ss.at[lin], fo_rs.at[me], k, c2)

    @pl.loop(0, F)
    def _(k):
        piece = at(k, rows, rows)
        for j in range(1, F):
            f2 = lax.rem(f + j, F)
            theirs = gated.at[piece, at(f2, CS, CS)]
            remote(theirs, theirs, gd_ss.at[k * F + f2], gd_rs.at[k * F + f2], f2, c).wait_recv()
        po[piece] = lax.dot_general(
            gated[piece], out_w[...], (((1,), (1,)), ((), ())), preferred_element_type=f32
        ).astype(bf16)
        for j in range(G):
            c2 = lax.rem(c + j, G)
            if j == 0:
                pl.when(k != f)(lambda: out_copy(k, c2).start())
            else:
                out_copy(k, c2).start()

    fin_in[me] = po[at(me, R, R)]
    for f2 in range(F):
        total = jnp.zeros((R, DB), f32)
        for c2 in range(G):
            lin = f2 * G + c2

            @pl.when(lin != me)
            def _():
                remote(po.at[at(lin, R, R)], fin_in.at[lin], fo_ss.at[lin], fo_rs.at[lin], f2, c2).wait_recv()

            total = total + fin_in[lin].astype(f32)
        out[:, f2 * DB : (f2 + 1) * DB] = total.astype(bf16)

    pl.loop(1, G)(lambda j: pp_copy(j).wait_send())
    for j in range(1, F):
        f2 = lax.rem(f + j, F)
        hid_copy(f2).wait_send()
        conv_copy(f2).wait_send()

        @pl.loop(0, F)
        def _(k):
            gate_copy(k, f2).wait_send()
            gated_copy(k, f2).wait_send()

    @pl.loop(1, N)
    def _(p):
        lin = lax.rem(me + p, N)
        pg_copy(lin // G, lax.rem(lin, G)).wait_send()
        out_copy(lin // G, lax.rem(lin, G)).wait_send()


def shards(F, G, *args):
    hidden, conv_out, state_in, gate_weight, xproj_weight, dt_weight, dt_bias, a_log, skip_gain, out_weight = args
    rows, channels = conv_out.shape
    depth, width = gate_weight.shape[0], hidden.shape[1]
    if rows % (16 * G) or channels % (LANES * F) or depth % LANES or width != depth * F:
        return generic_shards(*args)
    f32, bf16 = jnp.float32, jnp.bfloat16
    N, R, CS, L = F * G, rows // G, channels // F, rows * F
    wide = RANK + LANES
    span = STEPS * STATE
    dma = pltpu.SemaphoreType.DMA
    scratch = [
        pltpu.VMEM((rows, wide), f32),
        pltpu.VMEM((G, R, wide), f32),
        pltpu.VMEM((F, rows, CS), bf16),
        pltpu.VMEM((F, rows, depth), bf16),
        pltpu.VMEM((L, wide + LANES), bf16),
        pltpu.VMEM((F, L, CS), bf16),
        pltpu.VMEM((L, CS), f32),
        pltpu.VMEM((F, L, CS), bf16),
        pltpu.VMEM((rows, CS), f32),
        pltpu.VMEM((rows, CS), f32),
        pltpu.VMEM((rows, 4 * span), f32),
        pltpu.VMEM((L, CS), f32),
        pltpu.VMEM((L, channels), bf16),
        pltpu.VMEM((L, depth), bf16),
        pltpu.VMEM((N, R, depth), bf16),
    ]
    for count in (G, F, F, N, F * F, F * F, N):
        scratch += [dma((count,)), dma((count,))]
    return pl.pallas_call(
        functools.partial(fused_kernel, F, G),
        out_shape=jax.ShapeDtypeStruct((R, width), bf16),
        in_specs=[pl.BlockSpec(memory_space=pltpu.VMEM)] * 10,
        out_specs=pl.BlockSpec(memory_space=pltpu.VMEM),
        scratch_shapes=scratch,
        compiler_params=pltpu.CompilerParams(
            collective_id=0, has_side_effects=True, vmem_limit_bytes=48 * 2**20
        ),
    )(
        hidden,
        conv_out,
        state_in,
        gate_weight,
        xproj_weight,
        dt_weight,
        dt_bias[None],
        a_log,
        skip_gain[None],
        out_weight,
    )


def solution(mesh):
    placed = (
        P("fsdp", None),
        P("fsdp", "chan"),
        P("chan", None),
        P("fsdp", "chan"),
        P("chan", None),
        P(None, "chan"),
        P("chan"),
        P("chan", None),
        P("chan"),
        P("fsdp", "chan"),
    )
    return jax.shard_map(
        functools.partial(shards, mesh.shape["fsdp"], mesh.shape["chan"]), mesh=mesh, in_specs=placed, out_specs=P(("fsdp", "chan"), None), check_vma=False
    )
```

```python
import functools

import jax
import jax.numpy as jnp
from jax import lax
from jax.experimental import pallas as pl
from jax.experimental.pallas import tpu as pltpu
from jax.sharding import PartitionSpec as P

STATE = 16
RANK = 256
BLOCK = 16


def running_sum(values):
    lower = jnp.tril(jnp.ones((values.shape[0],) * 2, jnp.float32))
    return jnp.dot(lower, values, precision=lax.Precision.HIGHEST)


def generic_shards(
    hidden,
    conv_out,
    state_in,
    gate_weight,
    xproj_weight,
    dt_weight,
    dt_bias,
    a_log,
    skip_gain,
    out_weight,
):
    rows_here, channels = conv_out.shape
    partial_value = jnp.dot(conv_out, xproj_weight, preferred_element_type=jnp.float32)
    projected = lax.psum(partial_value, "chan")
    step_low = projected[:, :RANK].astype(jnp.bfloat16)
    in_coef = projected[:, RANK : RANK + STATE]
    out_coef = projected[:, RANK + STATE :]
    step_size = jax.nn.softplus(
        jnp.dot(step_low, dt_weight, preferred_element_type=jnp.float32) + dt_bias
    )
    decay_rate = -jnp.exp(a_log)
    inputs = conv_out.astype(jnp.float32)
    blocks = rows_here // BLOCK
    position_rows = lax.broadcasted_iota(jnp.int32, (BLOCK, BLOCK), 0)
    position_cols = lax.broadcasted_iota(jnp.int32, (BLOCK, BLOCK), 1)
    causal_mask = position_rows >= position_cols

    def block_step(carry_state, block_items):
        step_blk, input_blk, in_blk, out_blk = block_items
        within = running_sum(step_blk)
        spread = jnp.where(causal_mask[:, :, None], within[:, None, :] - within[None, :, :], 0.0)
        weights = jnp.where(
            causal_mask[:, :, None, None], jnp.exp(spread[:, :, :, None] * decay_rate), 0.0
        )
        driven = (step_blk * input_blk)[:, :, None] * in_blk[:, None, :]
        states = jnp.einsum("tscn,scn->tcn", weights, driven, precision=lax.Precision.HIGHEST)
        states = states + jnp.exp(within[:, :, None] * decay_rate) * carry_state[None]
        block_out = jnp.einsum("tcn,tn->tc", states, out_blk, precision=lax.Precision.HIGHEST)
        return (states[-1], block_out)

    def split_blocks(values):
        return values.reshape((blocks, BLOCK) + values.shape[1:])

    empty_state = jnp.zeros((channels, STATE), jnp.float32)
    last_state, local_out = lax.scan(
        block_step,
        empty_state,
        (
            split_blocks(step_size),
            split_blocks(inputs),
            split_blocks(in_coef),
            split_blocks(out_coef),
        ),
    )
    local_out = local_out.reshape((rows_here, channels))
    total_step = jnp.sum(step_size, axis=0)
    totals, finals = (
        lax.all_gather(total_step[None], "fsdp", axis=0, tiled=True),
        lax.all_gather(last_state[None], "fsdp", axis=0, tiled=True),
    )
    position = lax.axis_index("fsdp")
    sources = jnp.arange(totals.shape[0], dtype=jnp.int32)
    earlier_mask = sources < position
    through_sum = running_sum(totals)
    before_sum = jnp.sum(jnp.where(earlier_mask[:, None], totals, 0.0), axis=0)
    gap_steps = jnp.where(earlier_mask[:, None], before_sum[None, :] - through_sum, 0.0)
    factor = jnp.where(
        earlier_mask[:, None, None], jnp.exp(gap_steps[:, :, None] * decay_rate), 0.0
    )
    entering = (
        jnp.sum(factor * finals, axis=0) + jnp.exp(before_sum[:, None] * decay_rate) * state_in
    )
    through = running_sum(step_size)
    carried = jnp.einsum(
        "tcn,tn->tc",
        jnp.exp(through[:, :, None] * decay_rate) * entering[None],
        out_coef,
        precision=lax.Precision.HIGHEST,
    )
    scanned = local_out + carried
    gate_full, out_full = (
        lax.all_gather(gate_weight, "fsdp", axis=0, tiled=True),
        lax.all_gather(out_weight, "fsdp", axis=0, tiled=True),
    )
    gate_pre = jnp.dot(hidden, gate_full, preferred_element_type=jnp.float32)
    gated_out = ((scanned + skip_gain * inputs) * jax.nn.silu(gate_pre)).astype(jnp.bfloat16)
    summed = lax.psum_scatter(
        lax.dot_general(
            gated_out, out_full, (((1,), (1,)), ((), ())), preferred_element_type=jnp.float32
        ),
        "chan",
        scatter_dimension=0,
        tiled=True,
    )
    mixed = summed.astype(jnp.bfloat16)
    return mixed


LANES = 128
STEPS = 16


def fused_kernel(
    F,
    G,
    hidden,
    conv_h,
    state_h,
    gate_h,
    xproj_h,
    dt_h,
    dt_bias,
    a_log_h,
    skip,
    out_h,
    out,
    conv,
    state,
    gate_w,
    xproj,
    dt_w,
    a_log,
    out_w,
    load_sem,
    pp,
    pp_in,
    conv_in,
    hid_in,
    pg,
    gate_send,
    gate_own,
    gate_in,
    steps_s,
    drive_s,
    tiled_s,
    y_s,
    gated,
    po,
    ya_in,
    pair,
    zb_in,
    done,
    fc_in,
    pp_ss,
    pp_rs,
    cv_ss,
    cv_rs,
    hd_ss,
    hd_rs,
    pg_ss,
    pg_rs,
    pb_ss,
    pb_rs,
    gt_ss,
    gt_rs,
    gd_ss,
    gd_rs,
    gf_ss,
    ya_ss,
    ya_rs,
    zb_ss,
    zb_rs,
    fc_ss,
    fc_rs,
):
    f32, bf16 = jnp.float32, jnp.bfloat16
    N = F * G
    f, c = lax.axis_index("fsdp"), lax.axis_index("chan")
    me = f * G + c
    rows, channels = conv.shape
    R, CS, DB = rows // G, channels // F, gate_w.shape[0]
    H = G // 2
    mate = f + 1 - 2 * lax.rem(f, 2)
    c_mate = c + 1 - 2 * lax.rem(c, 2)
    peers = [lax.rem(f + j, F) for j in range(2, F, 2)]
    wide = pp.shape[1]

    def remote(src, dst, ss, rs, f2, c2):
        return pltpu.make_async_remote_copy(
            src_ref=src,
            dst_ref=dst,
            send_sem=ss,
            recv_sem=rs,
            device_id={"fsdp": f2, "chan": c2},
            device_id_type=pl.DeviceIdType.MESH,
        )

    def at(base, size, step):
        return pl.ds(pl.multiple_of(base * step, step), size)

    mine = at(f, CS, CS)
    loads = [
        pltpu.make_async_copy(src, dst, load_sem.at[i])
        for i, (src, dst) in enumerate(
            (
                (conv_h, conv),
                (xproj_h, xproj),
                (hidden.at[:, at(f, DB, DB)], hid_in.at[f]),
                (gate_h, gate_w),
                (dt_h.at[:, mine], dt_w),
                (a_log_h.at[:, mine], a_log),
                (state_h.at[:, mine], state),
                (out_h, out_w),
            )
        )
    ]
    for load in loads:
        load.start()
    barrier = pltpu.get_barrier_semaphore()

    @pl.loop(1, N)
    def _(p):
        lin = lax.rem(me + p, N)
        pl.semaphore_signal(
            barrier,
            inc=1,
            device_id={"fsdp": lin // G, "chan": lax.rem(lin, G)},
            device_id_type=pl.DeviceIdType.MESH,
        )

    pp[:, RANK:] = jnp.zeros((rows, wide - RANK), f32)
    loads[0].wait()
    loads[1].wait()
    pp[:, : xproj.shape[0]] = lax.dot_general(
        conv[...], xproj[...], (((1,), (1,)), ((), ())), preferred_element_type=f32
    )
    pl.semaphore_wait(barrier, N - 1)

    def pp_copy(j):
        c2 = lax.rem(c + j, G)
        return remote(pp.at[at(c2, R, R)], pp_in.at[c], pp_ss.at[c2], pp_rs.at[c], f, c2)

    def conv_copy(f2):
        return remote(conv.at[:, at(f2, CS, CS)], conv_in.at[f], cv_ss.at[f2], cv_rs.at[f], f2, c)

    def hid_copy(f2):
        return remote(hidden.at[:, at(f2, DB, DB)], hid_in.at[f], hd_ss.at[f2], hd_rs.at[f], f2, c)

    pl.loop(1, G)(lambda j: pp_copy(j).start())
    for j in range(1, F):
        hid_copy(lax.rem(f + j, F)).start()
        conv_copy(lax.rem(f + j, F)).start()
    conv_in[f] = conv[:, at(f, CS, CS)]
    loads[2].wait()
    loads[3].wait()

    def gate_copy(k, f2):
        piece = at(k, rows, rows)
        return remote(
            gate_send.at[f2, piece], gate_in.at[f, piece], gt_ss.at[k * F + f2], gt_rs.at[k * F + f], f2, c
        )

    def gate_block(k):
        piece = at(k, rows, rows)
        lhs = hid_in[k]
        for j in range(F):
            f2 = lax.rem(f + j, F)
            part = jnp.dot(lhs, gate_w[:, at(f2, CS, CS)], preferred_element_type=f32)
            if j == 0:
                gate_own[piece] = part
            else:
                gate_send[f2, piece] = part.astype(bf16)
                gate_copy(k, f2).start()

    gate_block(f)

    total = pp[at(c, R, R)]
    for j in range(1, G):
        c2 = lax.rem(c + j, G)
        remote(pp.at[at(c, R, R)], pp_in.at[c2], pp_ss.at[c2], pp_rs.at[c2], f, c2).wait_recv()
        total = total + pp_in[c2]
    high = total.astype(bf16)
    low = (total[:, RANK:] - high[:, RANK:].astype(f32)).astype(bf16)
    used = xproj.shape[0]
    pg[at(me, R, R)] = jnp.concatenate(
        [high[:, :used], low[:, : used - RANK], jnp.zeros((R, wide - 2 * used + RANK), bf16)], axis=1
    )

    def pg_copy(c2):
        rows_of = pg.at[at(me, R, R)]
        return remote(rows_of, rows_of, pg_ss.at[c2], pg_rs.at[c], f, c2)

    def pg_block(f2):
        rows_of = pg.at[at(f, rows, rows)]
        return remote(rows_of, rows_of, pb_ss.at[f2], pb_rs.at[f], f2, c)

    pl.loop(1, G)(lambda j: pg_copy(lax.rem(c + j, G)).start())

    @pl.loop(1, G)
    def _(j):
        c2 = lax.rem(c + j, G)
        there = pg.at[at(f * G + c2, R, R)]
        remote(there, there, pg_ss.at[c2], pg_rs.at[c2], f, c2).wait_recv()

    for j in range(1, F):
        pg_block(lax.rem(f + j, F)).start()
    for load in loads[4:]:
        load.wait()

    decay = -jnp.exp(a_log[...])
    bias = dt_bias[:, at(f, CS, CS)]
    gain = skip[:, at(f, CS, CS)]
    weight = dt_w[...]
    span = STEPS * STATE
    r_id = lax.broadcasted_iota(jnp.int32, (LANES, 4 * span), 0)
    q_id = lax.broadcasted_iota(jnp.int32, (LANES, 4 * span), 1)
    spread = (r_id == (q_id // span) * STATE + q_id % STATE).astype(bf16)
    own = (
        lax.broadcasted_iota(jnp.int32, (STEPS, span), 1) // STATE
        == lax.broadcasted_iota(jnp.int32, (STEPS, span), 0)
    )

    def scan_block(k, h):
        @pl.when(k != f)
        def _():
            there = pg.at[at(k, rows, rows)]
            remote(there, there, pb_ss.at[k], pb_rs.at[k], k, c).wait_recv()
            remote(conv.at[:, at(k, CS, CS)], conv_in.at[k], cv_ss.at[k], cv_rs.at[k], k, c).wait_recv()

        piece = at(k, rows, rows)
        raw = jnp.dot(pg[piece, :RANK], weight, preferred_element_type=f32) + bias
        size = jnp.maximum(raw, 0.0) + jnp.log1p(jnp.exp(-jnp.abs(raw)))
        steps_s[...] = size
        drive_s[...] = size * conv_in[k].astype(f32)
        tiled_s[...] = jnp.dot(pg[piece, RANK:], spread, preferred_element_type=f32)

        def sub(b, h):
            sl = at(b, STEPS, STEPS)
            dt = steps_s[sl]
            u = drive_s[sl]
            u_hi = u.astype(bf16)
            u_lo = (u - u_hi.astype(f32)).astype(bf16)

            def diagonal(i):
                return jnp.where(own, tiled_s[sl, i * span : (i + 1) * span], 0.0).astype(bf16)

            b_hi, c_hi, b_lo, c_lo = (diagonal(i) for i in range(4))
            driven = lax.dot_general(
                jnp.concatenate([b_hi, b_hi, b_lo], axis=0),
                jnp.concatenate([u_hi, u_lo, u_hi], axis=0),
                (((0,), (0,)), ((), ())),
                preferred_element_type=f32,
            )
            hs = []
            for s in range(STEPS):
                a = jnp.exp(dt[s : s + 1] * decay)
                h = a * h + driven[s * STATE : (s + 1) * STATE]
                hs.append(h.astype(bf16))
            both = jnp.dot(
                jnp.concatenate([c_hi, c_lo], axis=0),
                jnp.concatenate(hs, axis=0),
                preferred_element_type=f32,
            )
            y_s[at(k * (rows // STEPS) + b, STEPS, STEPS)] = both[:STEPS] + both[STEPS:]
            return h

        return lax.fori_loop(0, rows // STEPS, sub, h)

    def scan_and_gate(k, h):
        h = scan_block(k, h)

        @pl.when(k < F - 1)
        def _():
            g = lax.rem(f + 1 + k, F)
            remote(hidden.at[:, at(g, DB, DB)], hid_in.at[g], hd_ss.at[g], hd_rs.at[g], g, c).wait_recv()
            gate_block(g)

        return h

    lax.fori_loop(0, F, scan_and_gate, state[...])

    def gated_copy(k, f2):
        mine = gated.at[at(k, rows, rows), at(f, CS, CS)]
        return remote(mine, mine, gd_ss.at[k * F + f2], gd_rs.at[k * F + f], f2, c)

    @pl.loop(0, F)
    def _(k):
        piece = at(k, rows, rows)
        pre = gate_own[piece]
        for j in range(1, F):
            f2 = lax.rem(f + j, F)
            remote(
                gate_send.at[f2, piece], gate_in.at[f2, piece], gt_ss.at[k * F + f2], gt_rs.at[k * F + f2], f2, c
            ).wait_recv()
            pre = pre + gate_in[f2, piece].astype(f32)
        scanned = y_s[piece] + gain * conv_in[k].astype(f32)
        gated[piece, at(f, CS, CS)] = (scanned * (pre / (1.0 + jnp.exp(-pre)))).astype(bf16)
        for f2 in [mate] + peers:
            gated_copy(k, f2).start()

    def forward(k, f2):
        theirs = gated.at[at(k, rows, rows), at(f2, CS, CS)]
        return remote(theirs, theirs, gf_ss.at[k * F + f2], gd_rs.at[k * F + f2], mate, c)

    def gated_wait(k, f2):
        theirs = gated.at[at(k, rows, rows), at(f2, CS, CS)]
        remote(theirs, theirs, gd_ss.at[k * F + f2], gd_rs.at[k * F + f2], f2, c).wait_recv()

    def pass_on(k):
        for f2 in peers:
            gated_wait(k, f2)
            forward(k, f2).start()

    half, mine_z = lax.rem(c, 2), c // 2

    def ya_copy(k):
        return remote(po.at[k, :, 1 - half], ya_in.at[k], ya_ss.at[k], ya_rs.at[k], f, c_mate)

    def zb_copy(k, z):
        return remote(pair.at[k, z], zb_in.at[k, mine_z], zb_ss.at[k * H + z], zb_rs.at[k * H + mine_z], f, 2 * z + half)

    def fc_copy(k):
        return remote(done.at[k], fc_in.at[f], fc_ss.at[k], fc_rs.at[f], k, c)

    pass_on(0)

    @pl.loop(0, F + 2)
    def _(k):
        @pl.when(k + 1 < F)
        def _():
            pass_on(k + 1)

        @pl.when(k < F)
        def _():
            gated_wait(k, mate)
            for j in range(2, F, 2):
                gated_wait(k, lax.rem(mate + j, F))
            part = lax.dot_general(
                gated[at(k, rows, rows)], out_w[...], (((1,), (1,)), ((), ())), preferred_element_type=f32
            )
            po[k] = part.astype(bf16).reshape(H, 2, R, DB)
            ya_copy(k).start()

        @pl.when((k >= 1) & (k < F + 1))
        def _():
            q = k - 1
            ya_copy(q).wait_recv()
            pair[q] = (po[q, :, half].astype(f32) + ya_in[q].astype(f32)).astype(bf16)
            for j in range(1, H):
                zb_copy(q, lax.rem(mine_z + j, H)).start()

        @pl.when(k >= 2)
        def _():
            q = k - 2
            total = pair[q, mine_z].astype(f32)
            for j in range(1, H):
                z = lax.rem(mine_z + j, H)
                remote(pair.at[q, z], zb_in.at[q, z], zb_ss.at[q * H + z], zb_rs.at[q * H + z], f, 2 * z + half).wait_recv()
                total = total + zb_in[q, z].astype(f32)
            done[q] = total.astype(bf16)
            pl.when(q != f)(lambda: fc_copy(q).start())

    fc_in[f] = done[f]
    for f2 in range(F):
        @pl.when(f2 != f)
        def _():
            remote(done.at[f2], fc_in.at[f2], fc_ss.at[f2], fc_rs.at[f2], f2, c).wait_recv()

        out[:, f2 * DB : (f2 + 1) * DB] = fc_in[f2]

    pl.loop(1, G)(lambda j: pp_copy(j).wait_send())
    for j in range(1, F):
        f2 = lax.rem(f + j, F)
        hid_copy(f2).wait_send()
        conv_copy(f2).wait_send()

        @pl.loop(0, F)
        def _(k):
            gate_copy(k, f2).wait_send()

        pg_block(f2).wait_send()
        fc_copy(f2).wait_send()

    @pl.loop(0, F)
    def _(k):
        gated_copy(k, mate).wait_send()
        for f2 in peers:
            gated_copy(k, f2).wait_send()
            forward(k, f2).wait_send()
        ya_copy(k).wait_send()
        for j in range(1, H):
            zb_copy(k, lax.rem(mine_z + j, H)).wait_send()

    pl.loop(1, G)(lambda j: pg_copy(lax.rem(c + j, G)).wait_send())


def shards(F, G, *args):
    hidden, conv_out, state_in, gate_weight, xproj_weight, dt_weight, dt_bias, a_log, skip_gain, out_weight = args
    rows, channels = conv_out.shape
    depth, width = gate_weight.shape[0], hidden.shape[1]
    if G % 2 or F % 2 or rows % (16 * G) or channels % (LANES * F) or depth % LANES or width != depth * F:
        return generic_shards(*args)
    f32, bf16 = jnp.float32, jnp.bfloat16
    R, CS, L = rows // G, channels // F, rows * F
    wide = RANK + LANES
    span = STEPS * STATE
    dma = pltpu.SemaphoreType.DMA
    H = G // 2
    scratch = [
        pltpu.VMEM((rows, channels), bf16),
        pltpu.VMEM((STATE, CS), f32),
        pltpu.VMEM((depth, channels), bf16),
        pltpu.VMEM((xproj_weight.shape[1], channels), bf16),
        pltpu.VMEM((RANK, CS), bf16),
        pltpu.VMEM((STATE, CS), f32),
        pltpu.VMEM((depth, channels), bf16),
        dma((8,)),
        pltpu.VMEM((rows, wide), f32),
        pltpu.VMEM((G, R, wide), f32),
        pltpu.VMEM((F, rows, CS), bf16),
        pltpu.VMEM((F, rows, depth), bf16),
        pltpu.VMEM((L, wide), bf16),
        pltpu.VMEM((F, L, CS), bf16),
        pltpu.VMEM((L, CS), f32),
        pltpu.VMEM((F, L, CS), bf16),
        pltpu.VMEM((rows, CS), f32),
        pltpu.VMEM((rows, CS), f32),
        pltpu.VMEM((rows, 4 * span), f32),
        pltpu.VMEM((L, CS), f32),
        pltpu.VMEM((L, channels), bf16),
        pltpu.VMEM((F, H, 2, R, depth), bf16),
        pltpu.VMEM((F, H, R, depth), bf16),
        pltpu.VMEM((F, H, R, depth), bf16),
        pltpu.VMEM((F, H, R, depth), bf16),
        pltpu.VMEM((F, R, depth), bf16),
        pltpu.VMEM((F, R, depth), bf16),
    ]
    for count in (G, F, F, G, F, F * F, F * F):
        scratch += [dma((count,)), dma((count,))]
    scratch.append(dma((F * F,)))
    for count in (F, F * H, F):
        scratch += [dma((count,)), dma((count,))]
    in_vmem, in_hbm = pl.BlockSpec(memory_space=pltpu.VMEM), pl.BlockSpec(memory_space=pltpu.HBM)
    return pl.pallas_call(
        functools.partial(fused_kernel, F, G),
        out_shape=jax.ShapeDtypeStruct((R, width), bf16),
        in_specs=[in_hbm] * 6 + [in_vmem, in_hbm, in_vmem, in_hbm],
        out_specs=pl.BlockSpec(memory_space=pltpu.VMEM),
        scratch_shapes=scratch,
        compiler_params=pltpu.CompilerParams(
            collective_id=0, has_side_effects=True, vmem_limit_bytes=48 * 2**20
        ),
    )(
        hidden,
        conv_out,
        state_in.T,
        gate_weight,
        xproj_weight.T,
        dt_weight,
        dt_bias[None],
        a_log.T,
        skip_gain[None],
        out_weight,
    )


def solution(mesh):
    placed = (
        P("fsdp", None),
        P("fsdp", "chan"),
        P("chan", None),
        P("fsdp", "chan"),
        P("chan", None),
        P(None, "chan"),
        P("chan"),
        P("chan", None),
        P("chan"),
        P("fsdp", "chan"),
    )
    return jax.shard_map(
        functools.partial(shards, mesh.shape["fsdp"], mesh.shape["chan"]), mesh=mesh, in_specs=placed, out_specs=P(("fsdp", "chan"), None), check_vma=False
    )
```

```python
import functools

import jax
import jax.numpy as jnp
from jax import lax
from jax.experimental import pallas as pl
from jax.experimental.pallas import tpu as pltpu
from jax.sharding import PartitionSpec as P

STATE = 16
RANK = 256
BLOCK = 16


def running_sum(values):
    lower = jnp.tril(jnp.ones((values.shape[0],) * 2, jnp.float32))
    return jnp.dot(lower, values, precision=lax.Precision.HIGHEST)


def generic_shards(
    hidden,
    conv_out,
    state_in,
    gate_weight,
    xproj_weight,
    dt_weight,
    dt_bias,
    a_log,
    skip_gain,
    out_weight,
):
    rows_here, channels = conv_out.shape
    partial_value = jnp.dot(conv_out, xproj_weight, preferred_element_type=jnp.float32)
    projected = lax.psum(partial_value, "chan")
    step_low = projected[:, :RANK].astype(jnp.bfloat16)
    in_coef = projected[:, RANK : RANK + STATE]
    out_coef = projected[:, RANK + STATE :]
    step_size = jax.nn.softplus(
        jnp.dot(step_low, dt_weight, preferred_element_type=jnp.float32) + dt_bias
    )
    decay_rate = -jnp.exp(a_log)
    inputs = conv_out.astype(jnp.float32)
    blocks = rows_here // BLOCK
    position_rows = lax.broadcasted_iota(jnp.int32, (BLOCK, BLOCK), 0)
    position_cols = lax.broadcasted_iota(jnp.int32, (BLOCK, BLOCK), 1)
    causal_mask = position_rows >= position_cols

    def block_step(carry_state, block_items):
        step_blk, input_blk, in_blk, out_blk = block_items
        within = running_sum(step_blk)
        spread = jnp.where(causal_mask[:, :, None], within[:, None, :] - within[None, :, :], 0.0)
        weights = jnp.where(
            causal_mask[:, :, None, None], jnp.exp(spread[:, :, :, None] * decay_rate), 0.0
        )
        driven = (step_blk * input_blk)[:, :, None] * in_blk[:, None, :]
        states = jnp.einsum("tscn,scn->tcn", weights, driven, precision=lax.Precision.HIGHEST)
        states = states + jnp.exp(within[:, :, None] * decay_rate) * carry_state[None]
        block_out = jnp.einsum("tcn,tn->tc", states, out_blk, precision=lax.Precision.HIGHEST)
        return (states[-1], block_out)

    def split_blocks(values):
        return values.reshape((blocks, BLOCK) + values.shape[1:])

    empty_state = jnp.zeros((channels, STATE), jnp.float32)
    last_state, local_out = lax.scan(
        block_step,
        empty_state,
        (
            split_blocks(step_size),
            split_blocks(inputs),
            split_blocks(in_coef),
            split_blocks(out_coef),
        ),
    )
    local_out = local_out.reshape((rows_here, channels))
    total_step = jnp.sum(step_size, axis=0)
    totals, finals = (
        lax.all_gather(total_step[None], "fsdp", axis=0, tiled=True),
        lax.all_gather(last_state[None], "fsdp", axis=0, tiled=True),
    )
    position = lax.axis_index("fsdp")
    sources = jnp.arange(totals.shape[0], dtype=jnp.int32)
    earlier_mask = sources < position
    through_sum = running_sum(totals)
    before_sum = jnp.sum(jnp.where(earlier_mask[:, None], totals, 0.0), axis=0)
    gap_steps = jnp.where(earlier_mask[:, None], before_sum[None, :] - through_sum, 0.0)
    factor = jnp.where(
        earlier_mask[:, None, None], jnp.exp(gap_steps[:, :, None] * decay_rate), 0.0
    )
    entering = (
        jnp.sum(factor * finals, axis=0) + jnp.exp(before_sum[:, None] * decay_rate) * state_in
    )
    through = running_sum(step_size)
    carried = jnp.einsum(
        "tcn,tn->tc",
        jnp.exp(through[:, :, None] * decay_rate) * entering[None],
        out_coef,
        precision=lax.Precision.HIGHEST,
    )
    scanned = local_out + carried
    gate_full, out_full = (
        lax.all_gather(gate_weight, "fsdp", axis=0, tiled=True),
        lax.all_gather(out_weight, "fsdp", axis=0, tiled=True),
    )
    gate_pre = jnp.dot(hidden, gate_full, preferred_element_type=jnp.float32)
    gated_out = ((scanned + skip_gain * inputs) * jax.nn.silu(gate_pre)).astype(jnp.bfloat16)
    summed = lax.psum_scatter(
        lax.dot_general(
            gated_out, out_full, (((1,), (1,)), ((), ())), preferred_element_type=jnp.float32
        ),
        "chan",
        scatter_dimension=0,
        tiled=True,
    )
    mixed = summed.astype(jnp.bfloat16)
    return mixed


LANES = 128
STEPS = 16
LAGS = (0, 1, 1, 2, 3)


def fused_kernel(
    F,
    G,
    hidden,
    conv_h,
    state_h,
    gate_h,
    xproj_h,
    dt_h,
    dt_bias,
    a_log_h,
    skip,
    out_h,
    out,
    conv,
    state,
    gate_w,
    xproj,
    dt_w,
    a_log,
    out_w,
    load_sem,
    pp,
    pp_in,
    conv_in,
    hid_in,
    pg,
    gate_send,
    gate_own,
    gate_in,
    steps_s,
    drive_s,
    tiled_s,
    y_s,
    gated,
    po,
    ya_in,
    pair,
    zb_in,
    done,
    fc_in,
    pp_ss,
    pp_rs,
    cv_ss,
    cv_rs,
    hd_ss,
    hd_rs,
    pg_ss,
    pg_rs,
    pb_ss,
    pb_rs,
    gt_ss,
    gt_rs,
    gd_ss,
    gd_rs,
    gf_ss,
    ya_ss,
    ya_rs,
    zb_ss,
    zb_rs,
    fc_ss,
    fc_rs,
):
    f32, bf16 = jnp.float32, jnp.bfloat16
    f, c = lax.axis_index("fsdp"), lax.axis_index("chan")
    me = f * G + c
    rows, channels = conv.shape
    R, CS, DB = rows // G, channels // F, gate_w.shape[0]
    H = G // 2
    mate = f + 1 - 2 * lax.rem(f, 2)
    c_mate = c + 1 - 2 * lax.rem(c, 2)
    peers = [lax.rem(f + j, F) for j in range(2, F, 2)]
    mates = [lax.rem(mate + j, F) for j in range(2, F, 2)]
    wide = pp.shape[1]

    def remote(src, dst, ss, rs, f2, c2):
        return pltpu.make_async_remote_copy(
            src_ref=src,
            dst_ref=dst,
            send_sem=ss,
            recv_sem=rs,
            device_id={"fsdp": f2, "chan": c2},
            device_id_type=pl.DeviceIdType.MESH,
        )

    def at(base, size, step):
        return pl.ds(pl.multiple_of(base * step, step), size)

    mine = at(f, CS, CS)
    loads = [
        pltpu.make_async_copy(src, dst, load_sem.at[i])
        for i, (src, dst) in enumerate(
            (
                (conv_h, conv),
                (xproj_h, xproj),
                (hidden.at[:, at(f, DB, DB)], hid_in.at[f]),
                (gate_h, gate_w),
                (dt_h.at[:, mine], dt_w),
                (a_log_h.at[:, mine], a_log),
                (state_h.at[:, mine], state),
                (out_h, out_w),
            )
        )
    ]
    for load in loads:
        load.start()
    barrier = pltpu.get_barrier_semaphore()

    @pl.loop(1, G)
    def _(j):
        there = {"fsdp": f, "chan": lax.rem(c + j, G)}
        pl.semaphore_signal(barrier, inc=1, device_id=there, device_id_type=pl.DeviceIdType.MESH)

    for j in range(1, F):
        there = {"fsdp": lax.rem(f + j, F), "chan": c}
        pl.semaphore_signal(barrier, inc=1, device_id=there, device_id_type=pl.DeviceIdType.MESH)

    loads[0].wait()
    loads[1].wait()
    pp[:, : xproj.shape[0]] = lax.dot_general(
        conv[...], xproj[...], (((1,), (1,)), ((), ())), preferred_element_type=f32
    )
    pl.semaphore_wait(barrier, G + F - 2)

    def pp_copy(j):
        c2 = lax.rem(c + j, G)
        return remote(pp.at[at(c2, R, R)], pp_in.at[c], pp_ss.at[c2], pp_rs.at[c], f, c2)

    def conv_copy(f2):
        return remote(conv.at[:, at(f2, CS, CS)], conv_in.at[f], cv_ss.at[f2], cv_rs.at[f], f2, c)

    def hid_copy(f2):
        return remote(hidden.at[:, at(f2, DB, DB)], hid_in.at[f], hd_ss.at[f2], hd_rs.at[f], f2, c)

    pl.loop(1, G)(lambda j: pp_copy(j).start())
    for j in range(1, F):
        hid_copy(lax.rem(f + j, F)).start()
        conv_copy(lax.rem(f + j, F)).start()
    conv_in[f] = conv[:, at(f, CS, CS)]
    loads[2].wait()
    loads[3].wait()

    def gate_copy(k, f2):
        piece = at(k, rows, rows)
        return remote(
            gate_send.at[f2, piece], gate_in.at[f, piece], gt_ss.at[k * F + f2], gt_rs.at[k * F + f], f2, c
        )

    def gate_block(k):
        piece = at(k, rows, rows)
        lhs = hid_in[k]
        for j in range(F):
            f2 = lax.rem(f + j, F)
            part = jnp.dot(lhs, gate_w[:, at(f2, CS, CS)], preferred_element_type=f32)
            if j == 0:
                gate_own[piece] = part
            else:
                gate_send[f2, piece] = part.astype(bf16)
                gate_copy(k, f2).start()

    gate_block(f)

    total = pp[at(c, R, R)]
    for j in range(1, G):
        c2 = lax.rem(c + j, G)
        remote(pp.at[at(c, R, R)], pp_in.at[c2], pp_ss.at[c2], pp_rs.at[c2], f, c2).wait_recv()
        total = total + pp_in[c2]
    high = total.astype(bf16)
    low = (total[:, RANK:] - high[:, RANK:].astype(f32)).astype(bf16)
    used = xproj.shape[0]
    pg[at(me, R, R)] = jnp.concatenate(
        [high[:, :used], low[:, : used - RANK], jnp.zeros((R, wide - 2 * used + RANK), bf16)], axis=1
    )

    def pg_copy(c2):
        rows_of = pg.at[at(me, R, R)]
        return remote(rows_of, rows_of, pg_ss.at[c2], pg_rs.at[c], f, c2)

    def pg_block(f2):
        rows_of = pg.at[at(f, rows, rows)]
        return remote(rows_of, rows_of, pb_ss.at[f2], pb_rs.at[f], f2, c)

    pl.loop(1, G)(lambda j: pg_copy(lax.rem(c + j, G)).start())

    @pl.loop(1, G)
    def _(j):
        c2 = lax.rem(c + j, G)
        there = pg.at[at(f * G + c2, R, R)]
        remote(there, there, pg_ss.at[c2], pg_rs.at[c2], f, c2).wait_recv()

    for j in range(1, F):
        pg_block(lax.rem(f + j, F)).start()
    for g in [mate] + peers + mates:
        remote(hidden.at[:, at(g, DB, DB)], hid_in.at[g], hd_ss.at[g], hd_rs.at[g], g, c).wait_recv()
        gate_block(g)
    for load in loads[4:]:
        load.wait()

    decay = -jnp.exp(a_log[...])
    bias = dt_bias[:, at(f, CS, CS)]
    gain = skip[:, at(f, CS, CS)]
    weight = dt_w[...]
    span = STEPS * STATE
    r_id = lax.broadcasted_iota(jnp.int32, (LANES, 4 * span), 0)
    q_id = lax.broadcasted_iota(jnp.int32, (LANES, 4 * span), 1)
    spread = (r_id == (q_id // span) * STATE + q_id % STATE).astype(bf16)
    own = (
        lax.broadcasted_iota(jnp.int32, (STEPS, span), 1) // STATE
        == lax.broadcasted_iota(jnp.int32, (STEPS, span), 0)
    )

    def scan_block(k, h):
        @pl.when(k != f)
        def _():
            there = pg.at[at(k, rows, rows)]
            remote(there, there, pb_ss.at[k], pb_rs.at[k], k, c).wait_recv()
            remote(conv.at[:, at(k, CS, CS)], conv_in.at[k], cv_ss.at[k], cv_rs.at[k], k, c).wait_recv()

        piece = at(k, rows, rows)
        raw = jnp.dot(pg[piece, :RANK], weight, preferred_element_type=f32) + bias
        size = jnp.maximum(raw, 0.0) + jnp.log1p(jnp.exp(-jnp.abs(raw)))
        steps_s[...] = size
        drive_s[...] = size * conv_in[k].astype(f32)
        tiled_s[...] = jnp.dot(pg[piece, RANK:], spread, preferred_element_type=f32)

        def sub(b, h):
            sl = at(b, STEPS, STEPS)
            dt = steps_s[sl]
            u = drive_s[sl]
            u_hi = u.astype(bf16)
            u_lo = (u - u_hi.astype(f32)).astype(bf16)

            def diagonal(i):
                return jnp.where(own, tiled_s[sl, i * span : (i + 1) * span], 0.0).astype(bf16)

            b_hi, c_hi, b_lo, c_lo = (diagonal(i) for i in range(4))
            driven = lax.dot_general(
                jnp.concatenate([b_hi, b_hi, b_lo], axis=0),
                jnp.concatenate([u_hi, u_lo, u_hi], axis=0),
                (((0,), (0,)), ((), ())),
                preferred_element_type=f32,
            )
            hs = []
            for s in range(STEPS):
                a = jnp.exp(dt[s : s + 1] * decay)
                h = a * h + driven[s * STATE : (s + 1) * STATE]
                hs.append(h.astype(bf16))
            both = jnp.dot(
                jnp.concatenate([c_hi, c_lo], axis=0),
                jnp.concatenate(hs, axis=0),
                preferred_element_type=f32,
            )
            y_s[at(k * (rows // STEPS) + b, STEPS, STEPS)] = both[:STEPS] + both[STEPS:]
            return h

        return lax.fori_loop(0, rows // STEPS, sub, h)

    def gated_copy(k, f2):
        mine = gated.at[at(k, rows, rows), at(f, CS, CS)]
        return remote(mine, mine, gd_ss.at[k * F + f2], gd_rs.at[k * F + f], f2, c)

    def forward(k, f2):
        theirs = gated.at[at(k, rows, rows), at(f2, CS, CS)]
        return remote(theirs, theirs, gf_ss.at[k * F + f2], gd_rs.at[k * F + f2], mate, c)

    def gated_wait(k, f2):
        theirs = gated.at[at(k, rows, rows), at(f2, CS, CS)]
        remote(theirs, theirs, gd_ss.at[k * F + f2], gd_rs.at[k * F + f2], f2, c).wait_recv()

    def pass_on(k):
        for f2 in peers:
            gated_wait(k, f2)
            forward(k, f2).start()

    half, mine_z = lax.rem(c, 2), c // 2

    def ya_copy(k):
        return remote(po.at[k, :, 1 - half], ya_in.at[k], ya_ss.at[k], ya_rs.at[k], f, c_mate)

    def zb_copy(k, z):
        return remote(pair.at[k, z], zb_in.at[k, mine_z], zb_ss.at[k * H + z], zb_rs.at[k * H + mine_z], f, 2 * z + half)

    def fc_copy(k):
        return remote(done.at[k], fc_in.at[f], fc_ss.at[k], fc_rs.at[f], k, c)

    def gating(k):
        piece = at(k, rows, rows)
        pre = gate_own[piece]
        for j in range(1, F):
            f2 = lax.rem(f + j, F)
            remote(
                gate_send.at[f2, piece], gate_in.at[f2, piece], gt_ss.at[k * F + f2], gt_rs.at[k * F + f2], f2, c
            ).wait_recv()
            pre = pre + gate_in[f2, piece].astype(f32)
        scanned = y_s[piece] + gain * conv_in[k].astype(f32)
        gated[piece, at(f, CS, CS)] = (scanned * (pre / (1.0 + jnp.exp(-pre)))).astype(bf16)
        for f2 in [mate] + peers:
            gated_copy(k, f2).start()

    def partial_sums(k):
        for f2 in [mate] + mates:
            gated_wait(k, f2)
        part = lax.dot_general(
            gated[at(k, rows, rows)], out_w[...], (((1,), (1,)), ((), ())), preferred_element_type=f32
        )
        po[k] = part.astype(bf16).reshape(H, 2, R, DB)
        ya_copy(k).start()

    def pair_sums(k):
        ya_copy(k).wait_recv()
        pair[k] = (po[k, :, half].astype(f32) + ya_in[k].astype(f32)).astype(bf16)
        for j in range(1, H):
            zb_copy(k, lax.rem(mine_z + j, H)).start()

    def whole_sums(k):
        total = pair[k, mine_z].astype(f32)
        for j in range(1, H):
            z = lax.rem(mine_z + j, H)
            remote(pair.at[k, z], zb_in.at[k, z], zb_ss.at[k * H + z], zb_rs.at[k * H + z], f, 2 * z + half).wait_recv()
            total = total + zb_in[k, z].astype(f32)
        done[k] = total.astype(bf16)
        pl.when(k != f)(lambda: fc_copy(k).start())

    def stages(k, h):
        h = lax.cond(k < F, lambda: scan_block(k, h), lambda: h)
        for lag, stage in enumerate((gating, pass_on, partial_sums, pair_sums, whole_sums)):
            lag = LAGS[lag]

            @pl.when((k >= lag) & (k < F + lag))
            def _():
                stage(k - lag)

        return h

    lax.fori_loop(0, F + LAGS[-1], stages, state[...])

    fc_in[f] = done[f]
    for f2 in range(F):
        @pl.when(f2 != f)
        def _():
            remote(done.at[f2], fc_in.at[f2], fc_ss.at[f2], fc_rs.at[f2], f2, c).wait_recv()

        out[:, f2 * DB : (f2 + 1) * DB] = fc_in[f2]

    pl.loop(1, G)(lambda j: pp_copy(j).wait_send())
    for j in range(1, F):
        f2 = lax.rem(f + j, F)
        hid_copy(f2).wait_send()
        conv_copy(f2).wait_send()

        @pl.loop(0, F)
        def _(k):
            gate_copy(k, f2).wait_send()

        pg_block(f2).wait_send()
        fc_copy(f2).wait_send()

    @pl.loop(0, F)
    def _(k):
        gated_copy(k, mate).wait_send()
        for f2 in peers:
            gated_copy(k, f2).wait_send()
            forward(k, f2).wait_send()
        ya_copy(k).wait_send()
        for j in range(1, H):
            zb_copy(k, lax.rem(mine_z + j, H)).wait_send()

    pl.loop(1, G)(lambda j: pg_copy(lax.rem(c + j, G)).wait_send())


def shards(F, G, *args):
    hidden, conv_out, state_in, gate_weight, xproj_weight, dt_weight, dt_bias, a_log, skip_gain, out_weight = args
    rows, channels = conv_out.shape
    depth, width = gate_weight.shape[0], hidden.shape[1]
    if G % 2 or F % 2 or rows % (16 * G) or channels % (LANES * F) or depth % LANES or width != depth * F:
        return generic_shards(*args)
    f32, bf16 = jnp.float32, jnp.bfloat16
    R, CS, L = rows // G, channels // F, rows * F
    wide = RANK + LANES
    span = STEPS * STATE
    dma = pltpu.SemaphoreType.DMA
    H = G // 2
    scratch = [
        pltpu.VMEM((rows, channels), bf16),
        pltpu.VMEM((STATE, CS), f32),
        pltpu.VMEM((depth, channels), bf16),
        pltpu.VMEM((xproj_weight.shape[1], channels), bf16),
        pltpu.VMEM((RANK, CS), bf16),
        pltpu.VMEM((STATE, CS), f32),
        pltpu.VMEM((depth, channels), bf16),
        dma((8,)),
        pltpu.VMEM((rows, wide), f32),
        pltpu.VMEM((G, R, wide), f32),
        pltpu.VMEM((F, rows, CS), bf16),
        pltpu.VMEM((F, rows, depth), bf16),
        pltpu.VMEM((L, wide), bf16),
        pltpu.VMEM((F, L, CS), bf16),
        pltpu.VMEM((L, CS), f32),
        pltpu.VMEM((F, L, CS), bf16),
        pltpu.VMEM((rows, CS), f32),
        pltpu.VMEM((rows, CS), f32),
        pltpu.VMEM((rows, 4 * span), f32),
        pltpu.VMEM((L, CS), f32),
        pltpu.VMEM((L, channels), bf16),
        pltpu.VMEM((F, H, 2, R, depth), bf16),
        pltpu.VMEM((F, H, R, depth), bf16),
        pltpu.VMEM((F, H, R, depth), bf16),
        pltpu.VMEM((F, H, R, depth), bf16),
        pltpu.VMEM((F, R, depth), bf16),
        pltpu.VMEM((F, R, depth), bf16),
    ]
    for count in (G, F, F, G, F, F * F, F * F):
        scratch += [dma((count,)), dma((count,))]
    scratch.append(dma((F * F,)))
    for count in (F, F * H, F):
        scratch += [dma((count,)), dma((count,))]
    in_vmem, in_hbm = pl.BlockSpec(memory_space=pltpu.VMEM), pl.BlockSpec(memory_space=pltpu.HBM)
    return pl.pallas_call(
        functools.partial(fused_kernel, F, G),
        out_shape=jax.ShapeDtypeStruct((R, width), bf16),
        in_specs=[in_hbm] * 6 + [in_vmem, in_hbm, in_vmem, in_hbm],
        out_specs=pl.BlockSpec(memory_space=pltpu.VMEM),
        scratch_shapes=scratch,
        compiler_params=pltpu.CompilerParams(
            collective_id=0, has_side_effects=True, vmem_limit_bytes=48 * 2**20
        ),
    )(
        hidden,
        conv_out,
        state_in.T,
        gate_weight,
        xproj_weight.T,
        dt_weight,
        dt_bias[None],
        a_log.T,
        skip_gain[None],
        out_weight,
    )


def solution(mesh):
    placed = (
        P("fsdp", None),
        P("fsdp", "chan"),
        P("chan", None),
        P("fsdp", "chan"),
        P("chan", None),
        P(None, "chan"),
        P("chan"),
        P("chan", None),
        P("chan"),
        P("fsdp", "chan"),
    )
    return jax.shard_map(
        functools.partial(shards, mesh.shape["fsdp"], mesh.shape["chan"]), mesh=mesh, in_specs=placed, out_specs=P(("fsdp", "chan"), None), check_vma=False
    )
```

```python
import functools

import jax
import jax.numpy as jnp
from jax import lax
from jax.experimental import pallas as pl
from jax.experimental.pallas import tpu as pltpu
from jax.sharding import PartitionSpec as P

STATE = 16
RANK = 256
BLOCK = 16


def running_sum(values):
    lower = jnp.tril(jnp.ones((values.shape[0],) * 2, jnp.float32))
    return jnp.dot(lower, values, precision=lax.Precision.HIGHEST)


def generic_shards(
    hidden,
    conv_out,
    state_in,
    gate_weight,
    xproj_weight,
    dt_weight,
    dt_bias,
    a_log,
    skip_gain,
    out_weight,
):
    rows_here, channels = conv_out.shape
    partial_value = jnp.dot(conv_out, xproj_weight, preferred_element_type=jnp.float32)
    projected = lax.psum(partial_value, "chan")
    step_low = projected[:, :RANK].astype(jnp.bfloat16)
    in_coef = projected[:, RANK : RANK + STATE]
    out_coef = projected[:, RANK + STATE :]
    step_size = jax.nn.softplus(
        jnp.dot(step_low, dt_weight, preferred_element_type=jnp.float32) + dt_bias
    )
    decay_rate = -jnp.exp(a_log)
    inputs = conv_out.astype(jnp.float32)
    blocks = rows_here // BLOCK
    position_rows = lax.broadcasted_iota(jnp.int32, (BLOCK, BLOCK), 0)
    position_cols = lax.broadcasted_iota(jnp.int32, (BLOCK, BLOCK), 1)
    causal_mask = position_rows >= position_cols

    def block_step(carry_state, block_items):
        step_blk, input_blk, in_blk, out_blk = block_items
        within = running_sum(step_blk)
        spread = jnp.where(causal_mask[:, :, None], within[:, None, :] - within[None, :, :], 0.0)
        weights = jnp.where(
            causal_mask[:, :, None, None], jnp.exp(spread[:, :, :, None] * decay_rate), 0.0
        )
        driven = (step_blk * input_blk)[:, :, None] * in_blk[:, None, :]
        states = jnp.einsum("tscn,scn->tcn", weights, driven, precision=lax.Precision.HIGHEST)
        states = states + jnp.exp(within[:, :, None] * decay_rate) * carry_state[None]
        block_out = jnp.einsum("tcn,tn->tc", states, out_blk, precision=lax.Precision.HIGHEST)
        return (states[-1], block_out)

    def split_blocks(values):
        return values.reshape((blocks, BLOCK) + values.shape[1:])

    empty_state = jnp.zeros((channels, STATE), jnp.float32)
    last_state, local_out = lax.scan(
        block_step,
        empty_state,
        (
            split_blocks(step_size),
            split_blocks(inputs),
            split_blocks(in_coef),
            split_blocks(out_coef),
        ),
    )
    local_out = local_out.reshape((rows_here, channels))
    total_step = jnp.sum(step_size, axis=0)
    totals, finals = (
        lax.all_gather(total_step[None], "fsdp", axis=0, tiled=True),
        lax.all_gather(last_state[None], "fsdp", axis=0, tiled=True),
    )
    position = lax.axis_index("fsdp")
    sources = jnp.arange(totals.shape[0], dtype=jnp.int32)
    earlier_mask = sources < position
    through_sum = running_sum(totals)
    before_sum = jnp.sum(jnp.where(earlier_mask[:, None], totals, 0.0), axis=0)
    gap_steps = jnp.where(earlier_mask[:, None], before_sum[None, :] - through_sum, 0.0)
    factor = jnp.where(
        earlier_mask[:, None, None], jnp.exp(gap_steps[:, :, None] * decay_rate), 0.0
    )
    entering = (
        jnp.sum(factor * finals, axis=0) + jnp.exp(before_sum[:, None] * decay_rate) * state_in
    )
    through = running_sum(step_size)
    carried = jnp.einsum(
        "tcn,tn->tc",
        jnp.exp(through[:, :, None] * decay_rate) * entering[None],
        out_coef,
        precision=lax.Precision.HIGHEST,
    )
    scanned = local_out + carried
    gate_full, out_full = (
        lax.all_gather(gate_weight, "fsdp", axis=0, tiled=True),
        lax.all_gather(out_weight, "fsdp", axis=0, tiled=True),
    )
    gate_pre = jnp.dot(hidden, gate_full, preferred_element_type=jnp.float32)
    gated_out = ((scanned + skip_gain * inputs) * jax.nn.silu(gate_pre)).astype(jnp.bfloat16)
    summed = lax.psum_scatter(
        lax.dot_general(
            gated_out, out_full, (((1,), (1,)), ((), ())), preferred_element_type=jnp.float32
        ),
        "chan",
        scatter_dimension=0,
        tiled=True,
    )
    mixed = summed.astype(jnp.bfloat16)
    return mixed


LANES = 128
STEPS = 16
LAGS = (0, 1, 1, 2, 3)


def fused_kernel(
    F,
    G,
    hidden,
    conv_h,
    state_h,
    gate_h,
    xproj_h,
    dt_h,
    dt_bias,
    a_log_h,
    skip,
    out_h,
    out,
    conv,
    state,
    gate_w,
    xproj,
    dt_w,
    a_log,
    out_w,
    load_sem,
    pp,
    pp_in,
    conv_in,
    hid_in,
    pg,
    gate_send,
    gate_own,
    gate_in,
    steps_s,
    drive_s,
    tiled_s,
    y_s,
    gated,
    po,
    ya_in,
    pair,
    zb_in,
    done,
    fc_in,
    pp_ss,
    pp_rs,
    cv_ss,
    cv_rs,
    hd_ss,
    hd_rs,
    pg_ss,
    pg_rs,
    pb_ss,
    pb_rs,
    gt_ss,
    gt_rs,
    gd_ss,
    gd_rs,
    gf_ss,
    ya_ss,
    ya_rs,
    zb_ss,
    zb_rs,
    fc_ss,
    fc_rs,
):
    f32, bf16 = jnp.float32, jnp.bfloat16
    f, c = lax.axis_index("fsdp"), lax.axis_index("chan")
    me = f * G + c
    rows, channels = conv.shape
    R, CS, DB = rows // G, channels // F, gate_w.shape[0]
    H = G // 2
    mate = f + 1 - 2 * lax.rem(f, 2)
    c_mate = c + 1 - 2 * lax.rem(c, 2)
    peers = [lax.rem(f + j, F) for j in range(2, F, 2)]
    mates = [lax.rem(mate + j, F) for j in range(2, F, 2)]
    wide = pp.shape[1]

    def remote(src, dst, ss, rs, f2, c2):
        return pltpu.make_async_remote_copy(
            src_ref=src,
            dst_ref=dst,
            send_sem=ss,
            recv_sem=rs,
            device_id={"fsdp": f2, "chan": c2},
            device_id_type=pl.DeviceIdType.MESH,
        )

    def at(base, size, step):
        return pl.ds(pl.multiple_of(base * step, step), size)

    mine = at(f, CS, CS)
    loads = [
        pltpu.make_async_copy(src, dst, load_sem.at[i])
        for i, (src, dst) in enumerate(
            (
                (conv_h, conv),
                (xproj_h, xproj),
                (hidden.at[:, at(f, DB, DB)], hid_in.at[f]),
                (gate_h, gate_w),
                (dt_h.at[:, mine], dt_w),
                (a_log_h.at[:, mine], a_log),
                (state_h.at[:, mine], state),
                (out_h, out_w),
            )
        )
    ]
    for load in loads:
        load.start()
    barrier = pltpu.get_barrier_semaphore()

    @pl.loop(1, G)
    def _(j):
        there = {"fsdp": f, "chan": lax.rem(c + j, G)}
        pl.semaphore_signal(barrier, inc=1, device_id=there, device_id_type=pl.DeviceIdType.MESH)

    for j in range(1, F):
        there = {"fsdp": lax.rem(f + j, F), "chan": c}
        pl.semaphore_signal(barrier, inc=1, device_id=there, device_id_type=pl.DeviceIdType.MESH)

    loads[0].wait()
    loads[1].wait()
    pp[:, : xproj.shape[0]] = lax.dot_general(
        conv[...], xproj[...], (((1,), (1,)), ((), ())), preferred_element_type=f32
    )
    pl.semaphore_wait(barrier, G + F - 2)

    def pp_copy(j):
        c2 = lax.rem(c + j, G)
        return remote(pp.at[at(c2, R, R)], pp_in.at[c], pp_ss.at[c2], pp_rs.at[c], f, c2)

    def conv_copy(f2):
        return remote(conv.at[:, at(f2, CS, CS)], conv_in.at[f], cv_ss.at[f2], cv_rs.at[f], f2, c)

    def hid_copy(f2):
        return remote(hidden.at[:, at(f2, DB, DB)], hid_in.at[f], hd_ss.at[f2], hd_rs.at[f], f2, c)

    pl.loop(1, G)(lambda j: pp_copy(j).start())
    for j in range(1, F):
        hid_copy(lax.rem(f + j, F)).start()
        conv_copy(lax.rem(f + j, F)).start()
    conv_in[f] = conv[:, at(f, CS, CS)]
    loads[2].wait()
    loads[3].wait()

    def gate_copy(k, f2):
        piece = at(k, rows, rows)
        return remote(
            gate_send.at[f2, piece], gate_in.at[f, piece], gt_ss.at[k * F + f2], gt_rs.at[k * F + f], f2, c
        )

    def gate_block(k):
        piece = at(k, rows, rows)
        lhs = hid_in[k]
        for j in range(F):
            f2 = lax.rem(f + j, F)
            part = jnp.dot(lhs, gate_w[:, at(f2, CS, CS)], preferred_element_type=f32)
            if j == 0:
                gate_own[piece] = part
            else:
                gate_send[f2, piece] = part.astype(bf16)
                gate_copy(k, f2).start()

    gate_block(f)

    total = pp[at(c, R, R)]
    for j in range(1, G):
        c2 = lax.rem(c + j, G)
        remote(pp.at[at(c, R, R)], pp_in.at[c2], pp_ss.at[c2], pp_rs.at[c2], f, c2).wait_recv()
        total = total + pp_in[c2]
    high = total.astype(bf16)
    low = (total[:, RANK:] - high[:, RANK:].astype(f32)).astype(bf16)
    used = xproj.shape[0]
    pg[at(me, R, R)] = jnp.concatenate(
        [high[:, :used], low[:, : used - RANK], jnp.zeros((R, wide - 2 * used + RANK), bf16)], axis=1
    )

    def pg_copy(c2):
        rows_of = pg.at[at(me, R, R)]
        return remote(rows_of, rows_of, pg_ss.at[c2], pg_rs.at[c], f, c2)

    def pg_block(f2):
        rows_of = pg.at[at(f, rows, rows)]
        return remote(rows_of, rows_of, pb_ss.at[f2], pb_rs.at[f], f2, c)

    pl.loop(1, G)(lambda j: pg_copy(lax.rem(c + j, G)).start())

    @pl.loop(1, G)
    def _(j):
        c2 = lax.rem(c + j, G)
        there = pg.at[at(f * G + c2, R, R)]
        remote(there, there, pg_ss.at[c2], pg_rs.at[c2], f, c2).wait_recv()

    for j in range(1, F):
        pg_block(lax.rem(f + j, F)).start()
    for g in [mate] + peers + mates:
        remote(hidden.at[:, at(g, DB, DB)], hid_in.at[g], hd_ss.at[g], hd_rs.at[g], g, c).wait_recv()
        gate_block(g)
    for load in loads[4:]:
        load.wait()

    decay = -jnp.exp(a_log[...])
    bias = dt_bias[:, at(f, CS, CS)]
    gain = skip[:, at(f, CS, CS)]
    weight = dt_w[...]
    span = STEPS * STATE
    r_id = lax.broadcasted_iota(jnp.int32, (LANES, 4 * span), 0)
    q_id = lax.broadcasted_iota(jnp.int32, (LANES, 4 * span), 1)
    spread = (r_id == (q_id // span) * STATE + q_id % STATE).astype(bf16)
    own = (
        lax.broadcasted_iota(jnp.int32, (STEPS, span), 1) // STATE
        == lax.broadcasted_iota(jnp.int32, (STEPS, span), 0)
    )

    def scan_block(k, h):
        @pl.when(k != f)
        def _():
            there = pg.at[at(k, rows, rows)]
            remote(there, there, pb_ss.at[k], pb_rs.at[k], k, c).wait_recv()
            remote(conv.at[:, at(k, CS, CS)], conv_in.at[k], cv_ss.at[k], cv_rs.at[k], k, c).wait_recv()

        piece = at(k, rows, rows)
        raw = jnp.dot(pg[piece, :RANK], weight, preferred_element_type=f32) + bias
        size = jnp.maximum(raw, 0.0) + jnp.log1p(jnp.exp(-jnp.abs(raw)))
        steps_s[...] = size
        drive_s[...] = size * conv_in[k].astype(f32)
        tiled_s[...] = jnp.dot(pg[piece, RANK:], spread, preferred_element_type=f32)

        def sub(b, h):
            sl = at(b, STEPS, STEPS)
            dt = steps_s[sl]
            u = drive_s[sl]
            u_hi = u.astype(bf16)
            u_lo = (u - u_hi.astype(f32)).astype(bf16)

            def diagonal(i):
                return jnp.where(own, tiled_s[sl, i * span : (i + 1) * span], 0.0).astype(bf16)

            b_hi, c_hi, b_lo, c_lo = (diagonal(i) for i in range(4))
            driven = lax.dot_general(
                jnp.concatenate([b_hi, b_hi, b_lo], axis=0),
                jnp.concatenate([u_hi, u_lo, u_hi], axis=0),
                (((0,), (0,)), ((), ())),
                preferred_element_type=f32,
            )
            hs = []
            for s in range(STEPS):
                a = jnp.exp(dt[s : s + 1] * decay)
                h = a * h + driven[s * STATE : (s + 1) * STATE]
                hs.append(h.astype(bf16))
            both = jnp.dot(
                jnp.concatenate([c_hi, c_lo], axis=0),
                jnp.concatenate(hs, axis=0),
                preferred_element_type=f32,
            )
            y_s[at(k * (rows // STEPS) + b, STEPS, STEPS)] = both[:STEPS] + both[STEPS:]
            return h

        return lax.fori_loop(0, rows // STEPS, sub, h)

    def gated_copy(k, f2):
        mine = gated.at[at(k, rows, rows), at(f, CS, CS)]
        return remote(mine, mine, gd_ss.at[k * F + f2], gd_rs.at[k * F + f], f2, c)

    def forward(k, f2):
        theirs = gated.at[at(k, rows, rows), at(f2, CS, CS)]
        return remote(theirs, theirs, gf_ss.at[k * F + f2], gd_rs.at[k * F + f2], mate, c)

    def gated_wait(k, f2):
        theirs = gated.at[at(k, rows, rows), at(f2, CS, CS)]
        remote(theirs, theirs, gd_ss.at[k * F + f2], gd_rs.at[k * F + f2], f2, c).wait_recv()

    def pass_on(k):
        for f2 in peers:
            gated_wait(k, f2)
            forward(k, f2).start()

    half, mine_z = lax.rem(c, 2), c // 2

    def ya_copy(k):
        return remote(po.at[k, :, 1 - half], ya_in.at[k], ya_ss.at[k], ya_rs.at[k], f, c_mate)

    def zb_copy(k, z):
        return remote(pair.at[k, z], zb_in.at[k, mine_z], zb_ss.at[k * H + z], zb_rs.at[k * H + mine_z], f, 2 * z + half)

    def fc_copy(k):
        return remote(done.at[k], fc_in.at[f], fc_ss.at[k], fc_rs.at[f], k, c)

    def gating(k):
        piece = at(k, rows, rows)
        pre = gate_own[piece]
        for j in range(1, F):
            f2 = lax.rem(f + j, F)
            remote(
                gate_send.at[f2, piece], gate_in.at[f2, piece], gt_ss.at[k * F + f2], gt_rs.at[k * F + f2], f2, c
            ).wait_recv()
            pre = pre + gate_in[f2, piece].astype(f32)
        scanned = y_s[piece] + gain * conv_in[k].astype(f32)
        gated[piece, at(f, CS, CS)] = (scanned * (pre / (1.0 + jnp.exp(-pre)))).astype(bf16)
        for f2 in [mate] + peers:
            gated_copy(k, f2).start()

    def partial_sums(k):
        for f2 in [mate] + mates:
            gated_wait(k, f2)
        part = lax.dot_general(
            gated[at(k, rows, rows)], out_w[...], (((1,), (1,)), ((), ())), preferred_element_type=f32
        )
        po[k] = part.astype(bf16).reshape(H, 2, R, DB)
        ya_copy(k).start()

    def pair_sums(k):
        ya_copy(k).wait_recv()
        pair[k] = (po[k, :, half].astype(f32) + ya_in[k].astype(f32)).astype(bf16)
        for j in range(1, H):
            zb_copy(k, lax.rem(mine_z + j, H)).start()

    def whole_sums(k):
        total = pair[k, mine_z].astype(f32)
        for j in range(1, H):
            z = lax.rem(mine_z + j, H)
            remote(pair.at[k, z], zb_in.at[k, z], zb_ss.at[k * H + z], zb_rs.at[k * H + z], f, 2 * z + half).wait_recv()
            total = total + zb_in[k, z].astype(f32)
        done[k] = total.astype(bf16)
        pl.when(k != f)(lambda: fc_copy(k).start())

    def stages(k, h):
        h = lax.cond(k < F, lambda: scan_block(k, h), lambda: h)
        for lag, stage in enumerate((gating, pass_on, partial_sums, pair_sums, whole_sums)):
            lag = LAGS[lag]

            @pl.when((k >= lag) & (k < F + lag))
            def _():
                stage(k - lag)

        return h

    lax.fori_loop(0, F + LAGS[-1], stages, state[...])

    fc_in[f] = done[f]
    for f2 in range(F):
        @pl.when(f2 != f)
        def _():
            remote(done.at[f2], fc_in.at[f2], fc_ss.at[f2], fc_rs.at[f2], f2, c).wait_recv()

        out[:, f2 * DB : (f2 + 1) * DB] = fc_in[f2]

    pl.loop(1, G)(lambda j: pp_copy(j).wait_send())
    for j in range(1, F):
        f2 = lax.rem(f + j, F)
        hid_copy(f2).wait_send()
        conv_copy(f2).wait_send()

        @pl.loop(0, F)
        def _(k):
            gate_copy(k, f2).wait_send()

        pg_block(f2).wait_send()
        fc_copy(f2).wait_send()

    @pl.loop(0, F)
    def _(k):
        gated_copy(k, mate).wait_send()
        for f2 in peers:
            gated_copy(k, f2).wait_send()
            forward(k, f2).wait_send()
        ya_copy(k).wait_send()
        for j in range(1, H):
            zb_copy(k, lax.rem(mine_z + j, H)).wait_send()

    pl.loop(1, G)(lambda j: pg_copy(lax.rem(c + j, G)).wait_send())


def shards(F, G, *args):
    hidden, conv_out, state_in, gate_weight, xproj_weight, dt_weight, dt_bias, a_log, skip_gain, out_weight = args
    rows, channels = conv_out.shape
    depth, width = gate_weight.shape[0], hidden.shape[1]
    if G % 2 or F % 2 or rows % (16 * G) or channels % (LANES * F) or depth % LANES or width != depth * F:
        return generic_shards(*args)
    f32, bf16 = jnp.float32, jnp.bfloat16
    R, CS, L = rows // G, channels // F, rows * F
    wide = RANK + LANES
    span = STEPS * STATE
    dma = pltpu.SemaphoreType.DMA
    H = G // 2
    scratch = [
        pltpu.VMEM((rows, channels), bf16),
        pltpu.VMEM((STATE, CS), f32),
        pltpu.VMEM((depth, channels), bf16),
        pltpu.VMEM((xproj_weight.shape[1], channels), bf16),
        pltpu.VMEM((RANK, CS), bf16),
        pltpu.VMEM((STATE, CS), f32),
        pltpu.VMEM((depth, channels), bf16),
        dma((8,)),
        pltpu.VMEM((rows, wide), f32),
        pltpu.VMEM((G, R, wide), f32),
        pltpu.VMEM((F, rows, CS), bf16),
        pltpu.VMEM((F, rows, depth), bf16),
        pltpu.VMEM((L, wide), bf16),
        pltpu.VMEM((F, L, CS), bf16),
        pltpu.VMEM((L, CS), f32),
        pltpu.VMEM((F, L, CS), bf16),
        pltpu.VMEM((rows, CS), f32),
        pltpu.VMEM((rows, CS), f32),
        pltpu.VMEM((rows, 4 * span), f32),
        pltpu.VMEM((L, CS), f32),
        pltpu.VMEM((L, channels), bf16),
        pltpu.VMEM((F, H, 2, R, depth), bf16),
        pltpu.VMEM((F, H, R, depth), bf16),
        pltpu.VMEM((F, H, R, depth), bf16),
        pltpu.VMEM((F, H, R, depth), bf16),
        pltpu.VMEM((F, R, depth), bf16),
        pltpu.VMEM((F, R, depth), bf16),
    ]
    for count in (G, F, F, G, F, F * F, F * F):
        scratch += [dma((count,)), dma((count,))]
    scratch.append(dma((F * F,)))
    for count in (F, F * H, F):
        scratch += [dma((count,)), dma((count,))]
    in_vmem, in_hbm = pl.BlockSpec(memory_space=pltpu.VMEM), pl.BlockSpec(memory_space=pltpu.HBM)
    return pl.pallas_call(
        functools.partial(fused_kernel, F, G),
        out_shape=jax.ShapeDtypeStruct((R, width), bf16),
        in_specs=[in_hbm] * 6 + [in_vmem, in_hbm, in_vmem, in_hbm],
        out_specs=pl.BlockSpec(memory_space=pltpu.VMEM),
        scratch_shapes=scratch,
        compiler_params=pltpu.CompilerParams(
            collective_id=0, has_side_effects=True, vmem_limit_bytes=60 * 2**20
        ),
    )(
        hidden,
        conv_out,
        state_in.T,
        gate_weight,
        xproj_weight.T,
        dt_weight,
        dt_bias[None],
        a_log.T,
        skip_gain[None],
        out_weight,
    )


def solution(mesh):
    placed = (
        P("fsdp", None),
        P("fsdp", "chan"),
        P("chan", None),
        P("fsdp", "chan"),
        P("chan", None),
        P(None, "chan"),
        P("chan"),
        P("chan", None),
        P("chan"),
        P("fsdp", "chan"),
    )
    return jax.shard_map(
        functools.partial(shards, mesh.shape["fsdp"], mesh.shape["chan"]), mesh=mesh, in_specs=placed, out_specs=P(("fsdp", "chan"), None), check_vma=False
    )
```
